32 devices in a mesh: inp: 4 (over z), tm: 8 (over y, x, core).
Axes of the slice: x: 2, y: 2, z: 4, core: 2. Of those that a mesh axis runs over, the one named last changes fastest.
Arguments:
- samples: bfloat16 [512, 512, 1024], P('inp', 'tm'), may hold values from -6 to 6
- eq_gain: float32 [512, 512], P(None, 'inp'), may hold values from 0.5 to 2
Outputs:
- visibilities: float32 [512, 2, 512, 512], P(('inp', 'tm'))
The draws below stay inside these ranges and needn't reach their ends.
All inputs are finite; a program needn't handle non-finite values.
Results may differ from the reference program's by a relative error of at most 0.0033.
Values may be sent and summed in bfloat16 or wider, within the bound.
A program may use at most 256 MiB of HBM per device.

```python
import math
import jax
import jax.numpy as jnp
from jax import lax

INPUTS = 512
CHANNELS = 512
TAPS = 4
NFFT = 1024
FRAMES = 512


def shard_levels(key, shape, pieces, low, high):
    def one(axis_at, shards_of):
        draws = jax.random.uniform(jax.random.fold_in(jax.random.fold_in(key, 6), axis_at), (shards_of,), jnp.float32, low / len(pieces), high / len(pieces))
        return jnp.repeat(jnp.exp(draws), shape[axis_at] // shards_of).reshape((-1,) + (1,) * (len(shape) - axis_at - 1))

    loudness = one(*pieces[0])
    for cut in pieces[1:]:
        loudness = loudness * one(*cut)
    return loudness


def normal_values(rng, dims, width, most, split=(), kind=jnp.bfloat16):
    values = jax.random.normal(rng, dims, jnp.float32) * width
    if len(split) > 0:
        values = shard_levels(rng, dims, split, -0.22, 0.18) * values
    return jnp.clip(values, min=-most, max=most).astype(kind)


def setup_inputs(seed: int = 0) -> dict:
    arg_keys = jax.random.split(jax.random.key(seed), 3)
    return {
        "samples": normal_values(arg_keys[0], (INPUTS, FRAMES, NFFT), 1.0, 6.0, ((0, 4), (1, 8))),
        "eq_gain": jnp.clip(jnp.exp(math.log(2.0) - 1.3862944 * jax.random.uniform(arg_keys[1], (CHANNELS, INPUTS), jnp.float32) ** shard_levels(arg_keys[1], (CHANNELS, INPUTS), ((1, 4),), -0.2, 0.2)), 0.5, 2.0),
    }


def window_table(taps, nfft):
    position = jnp.arange(taps * nfft, dtype=jnp.int32).astype(jnp.float32) + 0.5
    shape_part = jnp.sinc(position / nfft - taps / 2.0)
    taper = 0.5 - 0.5 * jnp.cos(position * (2.0 * math.pi / (taps * nfft)))
    return (shape_part * taper).reshape(taps, nfft)

def fourier_table(channels, nfft):
    chan = jnp.arange(channels, dtype=jnp.int32)
    point = jnp.arange(nfft, dtype=jnp.int32)
    phase = (chan[:, None] * point[None, :] % nfft).astype(jnp.float32) * (2.0 * math.pi / nfft)
    scale = 1.0 / math.sqrt(nfft)
    table = jnp.stack([jnp.cos(phase) * scale, -jnp.sin(phase) * scale], axis=1)
    return table.reshape(2 * channels, nfft).astype(jnp.bfloat16)

def reference(samples, eq_gain):
    frames_all = samples.shape[1]
    nfft = samples.shape[2]
    channels = nfft // 2
    window = window_table(TAPS, nfft)
    table = fourier_table(channels, nfft)
    block = min(64, INPUTS)
    grouped = samples.reshape(INPUTS // block, block, frames_all, nfft)
    gains = eq_gain.T.reshape(INPUTS // block, block, channels)

    def channelize(pair):
        piece, gain = pair
        padded = jnp.concatenate([jnp.zeros((block, TAPS - 1, nfft), jnp.bfloat16), piece], axis=1)
        filtered = jnp.zeros((block, frames_all, nfft), jnp.float32)
        for tap in range(TAPS):
            filtered = filtered + window[tap] * padded[:, tap:tap + frames_all, :].astype(jnp.float32)
        filtered = filtered.astype(jnp.bfloat16)
        rows = filtered.reshape(block * frames_all, nfft)
        spectra = jnp.dot(rows, table.T, preferred_element_type=jnp.float32)
        spectra = spectra.reshape(block, frames_all, channels, 2) * gain[:, None, :, None]
        return spectra.astype(jnp.bfloat16)
    spectra = lax.map(channelize, (grouped, gains))
    spectra = spectra.reshape(INPUTS, frames_all, channels, 2).transpose(2, 3, 0, 1)

    def correlate(single):
        stacked = single.reshape(2 * INPUTS, frames_all)
        gram = jnp.dot(stacked, stacked.T, preferred_element_type=jnp.float32)
        real_part = (gram[:INPUTS, :INPUTS] + gram[INPUTS:, INPUTS:]) / frames_all
        imag_part = (gram[INPUTS:, :INPUTS] - gram[:INPUTS, INPUTS:]) / frames_all
        return jnp.stack([real_part, imag_part])
    return lax.map(correlate, spectra)
```

```python
import functools
import math

import jax
import jax.numpy as jnp
import numpy as np
from jax import lax
from jax.experimental import pallas as pl
from jax.experimental.pallas import tpu as pltpu
from jax.sharding import PartitionSpec as P

TAPS = 4
LANES = 128
STEP = 16


def passed_along(array, axis, by):
    devices = lax.axis_size(axis)
    pairs = [(i, i + by) for i in range(devices) if 0 <= i + by < devices]
    return lax.ppermute(array, axis, pairs)


def window_table(taps, nfft):
    position = np.arange(taps * nfft, dtype=np.float64) + 0.5
    shape_part = np.sinc(position / nfft - taps / 2.0)
    taper = 0.5 - 0.5 * np.cos(position * (2.0 * math.pi / (taps * nfft)))
    return (shape_part * taper).reshape(taps, nfft).astype(np.float32)


def fourier_table(channels, nfft):
    chan = np.arange(channels)
    point = np.arange(nfft)
    phase = (chan[:, None] * point[None, :] % nfft) * (2.0 * math.pi / nfft)
    scale = 1.0 / math.sqrt(nfft)
    table = np.stack([np.cos(phase) * scale, -np.sin(phase) * scale], axis=1)
    return table.reshape(2 * channels, nfft).astype(np.float32).astype(jnp.bfloat16)


def correlate_einsum(blocks, frames_all):
    groups_in = blocks.shape[0]
    count = blocks.shape[2]
    local_inputs = blocks.shape[4]
    inputs_all = groups_in * local_inputs
    gram = jnp.einsum("ptcraf,qtcsbf->crpasqb", blocks, blocks, preferred_element_type=jnp.float32)
    gram = gram.reshape(count, 2, inputs_all, 2, inputs_all)
    real_part = (gram[:, 0, :, 0, :] + gram[:, 1, :, 1, :]) / frames_all
    imag_part = (gram[:, 1, :, 0, :] - gram[:, 0, :, 1, :]) / frames_all
    return jnp.stack([real_part, imag_part], axis=1)


def plain_plan(samples, eq_gain):
    local_inputs, local_frames, nfft = samples.shape
    channels = nfft // 2
    n_inp = lax.axis_size("inp")
    n_time = lax.axis_size("tm")
    groups = n_inp * n_time
    chan_dev = channels // groups
    frames_all = n_time * local_frames
    tail = samples[:, local_frames - (TAPS - 1) :, :]
    before = passed_along(tail, "tm", 1)
    padded = jnp.concatenate([before, samples], axis=1)
    window = window_table(TAPS, nfft)
    filtered = jnp.zeros((local_inputs, local_frames, nfft), jnp.float32)
    for tap in range(TAPS):
        filtered = filtered + window[tap] * padded[:, tap : tap + local_frames, :].astype(
            jnp.float32
        )
    filtered = filtered.astype(jnp.bfloat16)
    table = jnp.asarray(fourier_table(channels, nfft))
    spectra = lax.dot_general(
        table, filtered, (((1,), (2,)), ((), ())), preferred_element_type=jnp.float32
    )
    spectra = spectra.reshape(channels, 2, local_inputs, local_frames) * eq_gain[:, None, :, None]
    spectra = spectra.astype(jnp.bfloat16)
    parcel = spectra.reshape(1, groups, chan_dev, 2, local_inputs, local_frames)
    arrived = lax.all_to_all(parcel, ("inp", "tm"), split_axis=1, concat_axis=0, tiled=True)
    count = arrived.shape[2]
    blocks = arrived.reshape(n_inp, n_time, count, 2, local_inputs, local_frames)
    return correlate_einsum(blocks, frames_all)


def spread_kernel(
    n_inp, n_time,
    x_hbm, before_ref, gain_ref, table_ref, window_ref,
    recv_hbm,
    xbuf, turned, taps_buf, history, filt, freq, send,
    load_sem, send_sem, recv_sem, own_sem,
):
    groups = n_inp * n_time
    inputs, frames, nfft = x_hbm.shape
    rows_all = table_ref.shape[0]
    rows_plane = rows_all // n_inp
    rows_dev = rows_all // groups
    pitch = freq.shape[0] // STEP
    steps = frames // STEP
    tiles = nfft // LANES
    z = lax.axis_index("inp")
    t = lax.axis_index("tm")
    me = z * n_time + t

    def load(step, slot):
        f0 = pl.multiple_of(step * STEP, STEP)
        return pltpu.make_async_copy(
            x_hbm.at[:, pl.ds(f0, STEP), :], xbuf.at[slot], load_sem.at[slot]
        )

    load(0, 0).start()
    barrier = pltpu.get_barrier_semaphore()

    @pl.loop(1, groups)
    def _(s):
        d = lax.rem(me + s, groups)
        pl.semaphore_signal(
            barrier, inc=1, device_id=(d // n_time, lax.rem(d, n_time)),
            device_id_type=pl.DeviceIdType.MESH,
        )

    history[...] = before_ref[...].astype(jnp.float32)

    def send_one(step, d_z, d_t):
        f0 = pl.multiple_of(step * STEP, STEP)
        d = d_z * n_time + d_t
        r0 = pl.multiple_of(d * rows_dev, rows_dev)
        pltpu.make_async_remote_copy(
            src_ref=send.at[pl.ds(r0, rows_dev), pl.ds(f0, STEP), :],
            dst_ref=recv_hbm.at[me, :, pl.ds(f0, STEP), :],
            send_sem=send_sem.at[d],
            recv_sem=recv_sem.at[me],
            device_id=(d_z, d_t),
            device_id_type=pl.DeviceIdType.MESH,
        ).start()

    def filter_step(slot):
        @pl.loop(0, tiles)
        def _(tile):
            lanes = pl.ds(pl.multiple_of(tile * LANES, LANES), LANES)
            turned[...] = (
                xbuf[slot, :, :, lanes].astype(jnp.float32).reshape(inputs * STEP, LANES)
            )
            taps_buf[0 : TAPS - 1] = history[:, :, lanes]
            for f in range(STEP):
                taps_buf[TAPS - 1 + f] = turned[pl.ds(f, inputs, stride=STEP), :]
            history[:, :, lanes] = taps_buf[STEP : STEP + TAPS - 1]
            for f in range(STEP):
                total = window_ref[0:1, lanes] * taps_buf[f]
                for tap in range(1, TAPS):
                    total = total + window_ref[tap : tap + 1, lanes] * taps_buf[f + tap]
                filt[f * inputs : (f + 1) * inputs, lanes] = total.astype(jnp.bfloat16)

    def transform(step, plane):
        f0 = pl.multiple_of(step * STEP, STEP)
        base = pl.multiple_of(plane * rows_plane, rows_plane)
        width = 4

        @pl.loop(0, STEP // width)
        def _(j):
            some = filt[pl.ds(pl.multiple_of(j * width * inputs, width * inputs), width * inputs), :]
            got = lax.dot_general(
                table_ref[pl.ds(base, rows_plane), :], some,
                (((1,), (1,)), ((), ())), preferred_element_type=jnp.float32,
            )
            for w in range(width):
                at = pl.multiple_of((j * width + w) * pitch, 8)
                freq[pl.ds(at, rows_plane), :] = got[:, w * inputs : (w + 1) * inputs]

        @pl.loop(0, rows_plane // 8)
        def _(i):
            for k in range(8):
                row = i * 8 + k
                chan = plane * (rows_plane // 2) + i * 4 + k // 2
                value = freq[pl.ds(row, STEP, stride=pitch), :] * gain_ref[pl.ds(chan, 1), :]
                send[base + row, pl.ds(f0, STEP), :] = value.astype(jnp.bfloat16)

    far = lax.rem(z + 2, 4)
    farther = 3 - z
    near = z + 1 - 2 * lax.rem(z, 2)

    @pl.loop(0, steps)
    def _(step):
        slot = lax.rem(step, 2)
        load(step, slot).wait()

        @pl.when(step + 1 < steps)
        def _():
            load(step + 1, 1 - slot).start()

        filter_step(slot)
        transform(step, far)

        @pl.when(step == 0)
        def _():
            pl.semaphore_wait(barrier, groups - 1)

        @pl.loop(0, n_time)
        def _(s):
            send_one(step, far, lax.rem(t + s, n_time))

            @pl.when((step > 0) & (s > 0))
            def _():
                send_one(step - 1, z, lax.rem(t + s, n_time))

        transform(step, near)
        transform(step, farther)

        @pl.loop(0, n_time)
        def _(s):
            send_one(step, farther, lax.rem(t + s, n_time))
            send_one(step, near, lax.rem(t + s, n_time))

        transform(step, z)

    @pl.loop(1, n_time)
    def _(s):
        send_one(steps - 1, z, lax.rem(t + s, n_time))

    own = pltpu.make_async_copy(
        send.at[pl.ds(pl.multiple_of(me * rows_dev, rows_dev), rows_dev)], recv_hbm.at[me], own_sem
    )
    own.start()
    own.wait()

    @pl.loop(1, groups)
    def _(s):
        d = lax.rem(me + s, groups)
        gone = send.at[pl.ds(pl.multiple_of(d * rows_dev, rows_dev), rows_dev)]
        pltpu.make_async_copy(gone, gone, send_sem.at[d]).wait()
        here = recv_hbm.at[d]
        pltpu.make_async_copy(here, here, recv_sem.at[d]).wait()


def spread(samples, before, eq_gain, n_inp, n_time):
    inputs, frames, nfft = samples.shape
    channels = nfft // 2
    rows = 2 * channels
    groups = n_inp * n_time
    pitch = rows // n_inp + 8
    vmem = pl.BlockSpec(memory_space=pltpu.VMEM)
    anywhere = pl.BlockSpec(memory_space=pl.ANY)
    return pl.pallas_call(
        functools.partial(spread_kernel, n_inp, n_time),
        out_shape=jax.ShapeDtypeStruct((groups, rows // groups, frames, inputs), jnp.bfloat16),
        in_specs=[anywhere, vmem, vmem, vmem, vmem],
        out_specs=anywhere,
        scratch_shapes=[
            pltpu.VMEM((2, inputs, STEP, nfft), jnp.bfloat16),
            pltpu.VMEM((inputs * STEP, LANES), jnp.float32),
            pltpu.VMEM((STEP + TAPS - 1, inputs, LANES), jnp.float32),
            pltpu.VMEM((TAPS - 1, inputs, nfft), jnp.float32),
            pltpu.VMEM((STEP * inputs, nfft), jnp.bfloat16),
            pltpu.VMEM((STEP * pitch, LANES), jnp.float32),
            pltpu.VMEM((rows, frames, inputs), jnp.bfloat16),
            pltpu.SemaphoreType.DMA((2,)),
            pltpu.SemaphoreType.DMA((groups,)),
            pltpu.SemaphoreType.DMA((groups,)),
            pltpu.SemaphoreType.DMA,
        ],
        compiler_params=pltpu.CompilerParams(
            collective_id=0, has_side_effects=True, vmem_limit_bytes=56 * 1024 * 1024
        ),
        cost_estimate=pl.CostEstimate(
            flops=2 * rows * nfft * inputs * frames,
            bytes_accessed=4 * inputs * frames * nfft,
            transcendentals=0,
        ),
        name="filter_transform_spread",
    )(
        samples, before, eq_gain,
        jnp.asarray(fourier_table(channels, nfft)), jnp.asarray(window_table(TAPS, nfft)),
    )


def correlate_kernel(n_inp, scale, block_ref, out_ref):
    sources, _, frames, inputs = block_ref.shape
    n_time = sources // n_inp

    def part(r):
        pieces = [
            block_ref[p * n_time : (p + 1) * n_time, r].reshape(n_time * frames, inputs)
            for p in range(n_inp)
        ]
        return jnp.concatenate(pieces, axis=1)

    real, imag = part(0), part(1)
    real_t, imag_t = real.T, imag.T
    right = jnp.concatenate([real, imag], axis=0)
    left = jnp.concatenate([real_t, imag_t], axis=1)
    out_ref[0, 0] = jnp.dot(left, right, preferred_element_type=jnp.float32) * scale
    left = jnp.concatenate([imag_t, -real_t], axis=1)
    out_ref[0, 1] = jnp.dot(left, right, preferred_element_type=jnp.float32) * scale


def correlate(arrived, n_inp):
    sources, rows, frames, inputs = arrived.shape
    count = rows // 2
    inputs_all = n_inp * inputs
    frames_all = sources // n_inp * frames
    return pl.pallas_call(
        functools.partial(correlate_kernel, n_inp, 1.0 / frames_all),
        grid=(count,),
        out_shape=jax.ShapeDtypeStruct((count, 2, inputs_all, inputs_all), jnp.float32),
        in_specs=[pl.BlockSpec((sources, 2, frames, inputs), lambda c: (0, c, 0, 0))],
        out_specs=pl.BlockSpec((1, 2, inputs_all, inputs_all), lambda c: (c, 0, 0, 0)),
        compiler_params=pltpu.CompilerParams(vmem_limit_bytes=48 * 1024 * 1024),
        cost_estimate=pl.CostEstimate(
            flops=count * 8 * inputs_all * inputs_all * frames_all,
            bytes_accessed=arrived.size * 2 + count * 8 * inputs_all * inputs_all,
            transcendentals=0,
        ),
        name="correlate",
    )(arrived)


def on_device(samples, eq_gain):
    local_inputs, local_frames, nfft = samples.shape
    n_inp = lax.axis_size("inp")
    n_time = lax.axis_size("tm")
    if local_inputs != LANES or n_inp != 4 or n_time != 8 or local_frames % STEP:
        return plain_plan(samples, eq_gain)
    tail = jnp.swapaxes(samples[:, local_frames - (TAPS - 1) :, :], 0, 1)
    before = passed_along(tail, "tm", 1)
    arrived = spread(samples, before, eq_gain, n_inp, n_time)
    return correlate(arrived, n_inp)


def solution(mesh):
    placed = (P("inp", "tm", None), P(None, "inp"))
    return jax.shard_map(
        on_device,
        mesh=mesh,
        in_specs=placed,
        out_specs=P(("inp", "tm"), None, None, None),
        check_vma=False,
    )
```

```python
import functools
import math

import jax
import jax.numpy as jnp
import numpy as np
from jax import lax
from jax.experimental import pallas as pl
from jax.experimental.pallas import tpu as pltpu
from jax.sharding import PartitionSpec as P

TAPS = 4
LANES = 128
STEP = 16


def passed_along(array, axis, by):
    devices = lax.axis_size(axis)
    pairs = [(i, i + by) for i in range(devices) if 0 <= i + by < devices]
    return lax.ppermute(array, axis, pairs)


def window_table(taps, nfft):
    position = np.arange(taps * nfft, dtype=np.float64) + 0.5
    shape_part = np.sinc(position / nfft - taps / 2.0)
    taper = 0.5 - 0.5 * np.cos(position * (2.0 * math.pi / (taps * nfft)))
    return (shape_part * taper).reshape(taps, nfft).astype(np.float32)


def fourier_table(channels, nfft):
    chan = np.arange(channels)
    point = np.arange(nfft)
    phase = (chan[:, None] * point[None, :] % nfft) * (2.0 * math.pi / nfft)
    scale = 1.0 / math.sqrt(nfft)
    table = np.stack([np.cos(phase) * scale, -np.sin(phase) * scale], axis=1)
    return table.reshape(2 * channels, nfft).astype(np.float32).astype(jnp.bfloat16)


def correlate_einsum(blocks, frames_all):
    groups_in = blocks.shape[0]
    count = blocks.shape[2]
    local_inputs = blocks.shape[4]
    inputs_all = groups_in * local_inputs
    gram = jnp.einsum("ptcraf,qtcsbf->crpasqb", blocks, blocks, preferred_element_type=jnp.float32)
    gram = gram.reshape(count, 2, inputs_all, 2, inputs_all)
    real_part = (gram[:, 0, :, 0, :] + gram[:, 1, :, 1, :]) / frames_all
    imag_part = (gram[:, 1, :, 0, :] - gram[:, 0, :, 1, :]) / frames_all
    return jnp.stack([real_part, imag_part], axis=1)


def plain_plan(samples, eq_gain):
    local_inputs, local_frames, nfft = samples.shape
    channels = nfft // 2
    n_inp = lax.axis_size("inp")
    n_time = lax.axis_size("tm")
    groups = n_inp * n_time
    chan_dev = channels // groups
    frames_all = n_time * local_frames
    tail = samples[:, local_frames - (TAPS - 1) :, :]
    before = passed_along(tail, "tm", 1)
    padded = jnp.concatenate([before, samples], axis=1)
    window = window_table(TAPS, nfft)
    filtered = jnp.zeros((local_inputs, local_frames, nfft), jnp.float32)
    for tap in range(TAPS):
        filtered = filtered + window[tap] * padded[:, tap : tap + local_frames, :].astype(
            jnp.float32
        )
    filtered = filtered.astype(jnp.bfloat16)
    table = jnp.asarray(fourier_table(channels, nfft))
    spectra = lax.dot_general(
        table, filtered, (((1,), (2,)), ((), ())), preferred_element_type=jnp.float32
    )
    spectra = spectra.reshape(channels, 2, local_inputs, local_frames) * eq_gain[:, None, :, None]
    spectra = spectra.astype(jnp.bfloat16)
    parcel = spectra.reshape(1, groups, chan_dev, 2, local_inputs, local_frames)
    arrived = lax.all_to_all(parcel, ("inp", "tm"), split_axis=1, concat_axis=0, tiled=True)
    count = arrived.shape[2]
    blocks = arrived.reshape(n_inp, n_time, count, 2, local_inputs, local_frames)
    return correlate_einsum(blocks, frames_all)


def spread_kernel(
    n_inp, n_time,
    x_hbm, gain_ref, table_ref, window_ref,
    recv_hbm,
    xbuf, turned, tail, taps_buf, halo_out, halo_in, filt, freq, send,
    load_sem, send_sem, recv_sem, halo_send_sem, halo_recv_sem, own_sem,
):
    groups = n_inp * n_time
    inputs, frames, nfft = x_hbm.shape
    rows_all = table_ref.shape[0]
    rows_plane = rows_all // n_inp
    rows_dev = rows_all // groups
    pitch = freq.shape[0] // STEP
    steps = frames // STEP
    tiles = nfft // LANES
    keep = TAPS - 1
    z = lax.axis_index("inp")
    t = lax.axis_index("tm")
    me = z * n_time + t

    def load(step):
        f0 = pl.multiple_of(step * STEP, STEP)
        slot = lax.rem(step, 2)
        return pltpu.make_async_copy(
            x_hbm.at[:, pl.ds(f0, STEP), :], xbuf.at[slot], load_sem.at[slot]
        )

    load(steps - 1).start()
    load(steps - 2).start()
    barrier = pltpu.get_barrier_semaphore()

    @pl.loop(1, groups)
    def _(s):
        d = lax.rem(me + s, groups)
        pl.semaphore_signal(
            barrier, inc=1, device_id=(d // n_time, lax.rem(d, n_time)),
            device_id_type=pl.DeviceIdType.MESH,
        )

    def send_one(step, d_z, s):
        d_t = lax.rem(t + s, n_time)
        f0 = pl.multiple_of(step * STEP, STEP)
        d = d_z * n_time + d_t
        r0 = pl.multiple_of(d * rows_dev, rows_dev)
        pltpu.make_async_remote_copy(
            src_ref=send.at[pl.ds(r0, rows_dev), pl.ds(f0, STEP), :],
            dst_ref=recv_hbm.at[me, :, pl.ds(f0, STEP), :],
            send_sem=send_sem.at[d],
            recv_sem=recv_sem.at[me],
            device_id=(d_z, d_t),
            device_id_type=pl.DeviceIdType.MESH,
        ).start()

    def halo():
        return pltpu.make_async_remote_copy(
            src_ref=halo_out,
            dst_ref=halo_in,
            send_sem=halo_send_sem,
            recv_sem=halo_recv_sem,
            device_id=(z, lax.rem(t + 1, n_time)),
            device_id_type=pl.DeviceIdType.MESH,
        )

    def filter_step(step):
        slot = lax.rem(step, 2)

        @pl.loop(0, tiles)
        def _(tile):
            lanes = pl.ds(pl.multiple_of(tile * LANES, LANES), LANES)
            turned[...] = (
                xbuf[slot, :, :, lanes].astype(jnp.float32).reshape(inputs * STEP, LANES)
            )

            @pl.when(step > 0)
            def _():
                earlier = xbuf[1 - slot, :, :, lanes].astype(jnp.float32)[:, STEP - 8 :, :]
                tail[...] = earlier.reshape(inputs * 8, LANES)
                for k in range(keep):
                    taps_buf[k] = tail[pl.ds(8 - keep + k, inputs, stride=8), :]

            @pl.when(step == 0)
            def _():
                taps_buf[0:keep] = halo_in[:, :, lanes].astype(jnp.float32)

            for f in range(STEP):
                taps_buf[keep + f] = turned[pl.ds(f, inputs, stride=STEP), :]

            @pl.when(step == steps - 1)
            def _():
                halo_out[:, :, lanes] = taps_buf[STEP : STEP + keep].astype(jnp.bfloat16)

            for f in range(STEP):
                total = window_ref[0:1, lanes] * taps_buf[f]
                for tap in range(1, TAPS):
                    total = total + window_ref[tap : tap + 1, lanes] * taps_buf[f + tap]
                filt[f * inputs : (f + 1) * inputs, lanes] = total.astype(jnp.bfloat16)

    def transform(step, plane):
        f0 = pl.multiple_of(step * STEP, STEP)
        base = pl.multiple_of(plane * rows_plane, rows_plane)
        width = 4

        @pl.loop(0, STEP // width)
        def _(j):
            some = filt[pl.ds(pl.multiple_of(j * width * inputs, width * inputs), width * inputs), :]
            got = lax.dot_general(
                table_ref[pl.ds(base, rows_plane), :], some,
                (((1,), (1,)), ((), ())), preferred_element_type=jnp.float32,
            )
            for w in range(width):
                at = pl.multiple_of((j * width + w) * pitch, 8)
                freq[pl.ds(at, rows_plane), :] = got[:, w * inputs : (w + 1) * inputs]

        @pl.loop(0, rows_plane // 8)
        def _(i):
            for k in range(8):
                row = i * 8 + k
                chan = plane * (rows_plane // 2) + i * 4 + k // 2
                value = freq[pl.ds(row, STEP, stride=pitch), :] * gain_ref[pl.ds(chan, 1), :]
                send[base + row, pl.ds(f0, STEP), :] = value.astype(jnp.bfloat16)

    far = lax.rem(z + 2, 4)
    farther = 3 - z
    near = z + 1 - 2 * lax.rem(z, 2)
    half = n_time // 2

    @pl.loop(0, steps)
    def _(turn):
        step = steps - 1 - turn

        @pl.when(turn == 0)
        def _():
            load(steps - 1).wait()

        @pl.when(step > 0)
        def _():
            load(step - 1).wait()

        @pl.when(step == 0)
        def _():
            @pl.when(t > 0)
            def _():
                halo().wait_recv()

            @pl.when(t == 0)
            def _():
                halo_in[...] = jnp.zeros_like(halo_in)

        filter_step(step)

        @pl.when(step > 1)
        def _():
            load(step - 2).start()

        transform(step, far)

        @pl.when(turn == 0)
        def _():
            pl.semaphore_wait(barrier, groups - 1)

            @pl.when(t < n_time - 1)
            def _():
                halo().start()

        @pl.loop(0, half)
        def _(s):
            send_one(step, far, s)

        transform(step, z)

        @pl.loop(0, half)
        def _(s):
            send_one(step, far, s + half)
            send_one(step, z, s + half)

            @pl.when(s > 0)
            def _():
                send_one(step, z, s)

        transform(step, near)
        transform(step, farther)

        @pl.loop(0, n_time)
        def _(s):
            send_one(step, near, s)
            send_one(step, farther, s)

    own = pltpu.make_async_copy(
        send.at[pl.ds(pl.multiple_of(me * rows_dev, rows_dev), rows_dev)], recv_hbm.at[me], own_sem
    )
    own.start()
    own.wait()

    @pl.when(t < n_time - 1)
    def _():
        halo().wait_send()

    @pl.loop(1, groups)
    def _(s):
        d = lax.rem(me + s, groups)
        gone = send.at[pl.ds(pl.multiple_of(d * rows_dev, rows_dev), rows_dev)]
        pltpu.make_async_copy(gone, gone, send_sem.at[d]).wait()
        here = recv_hbm.at[d]
        pltpu.make_async_copy(here, here, recv_sem.at[d]).wait()


def spread(samples, eq_gain, n_inp, n_time):
    inputs, frames, nfft = samples.shape
    channels = nfft // 2
    rows = 2 * channels
    groups = n_inp * n_time
    pitch = rows // n_inp + 8
    vmem = pl.BlockSpec(memory_space=pltpu.VMEM)
    anywhere = pl.BlockSpec(memory_space=pl.ANY)
    return pl.pallas_call(
        functools.partial(spread_kernel, n_inp, n_time),
        out_shape=jax.ShapeDtypeStruct((groups, rows // groups, frames, inputs), jnp.bfloat16),
        in_specs=[anywhere, vmem, vmem, vmem],
        out_specs=anywhere,
        scratch_shapes=[
            pltpu.VMEM((2, inputs, STEP, nfft), jnp.bfloat16),
            pltpu.VMEM((inputs * STEP, LANES), jnp.float32),
            pltpu.VMEM((inputs * 8, LANES), jnp.float32),
            pltpu.VMEM((STEP + TAPS - 1, inputs, LANES), jnp.float32),
            pltpu.VMEM((TAPS - 1, inputs, nfft), jnp.bfloat16),
            pltpu.VMEM((TAPS - 1, inputs, nfft), jnp.bfloat16),
            pltpu.VMEM((STEP * inputs, nfft), jnp.bfloat16),
            pltpu.VMEM((STEP * pitch, LANES), jnp.float32),
            pltpu.VMEM((rows, frames, inputs), jnp.bfloat16),
            pltpu.SemaphoreType.DMA((2,)),
            pltpu.SemaphoreType.DMA((groups,)),
            pltpu.SemaphoreType.DMA((groups,)),
            pltpu.SemaphoreType.DMA,
            pltpu.SemaphoreType.DMA,
            pltpu.SemaphoreType.DMA,
        ],
        compiler_params=pltpu.CompilerParams(
            collective_id=0, has_side_effects=True, vmem_limit_bytes=56 * 1024 * 1024
        ),
        cost_estimate=pl.CostEstimate(
            flops=2 * rows * nfft * inputs * frames,
            bytes_accessed=4 * inputs * frames * nfft,
            transcendentals=0,
        ),
        name="filter_transform_spread",
    )(
        samples, eq_gain,
        jnp.asarray(fourier_table(channels, nfft)), jnp.asarray(window_table(TAPS, nfft)),
    )


def correlate_kernel(n_inp, scale, block_ref, out_ref):
    sources, rows, frames, inputs = block_ref.shape
    n_time = sources // n_inp
    half = n_inp * inputs // 2

    def part(row):
        pieces = [
            block_ref[p * n_time : (p + 1) * n_time, row].reshape(n_time * frames, inputs)
            for p in range(n_inp)
        ]
        return jnp.concatenate(pieces, axis=1)

    for chan in range(rows // 2):
        real, imag = part(2 * chan), part(2 * chan + 1)
        real_t, imag_t = real.T, imag.T
        right = jnp.concatenate([real, imag], axis=0)
        for kind, left in enumerate(
            [
                jnp.concatenate([real_t, imag_t], axis=1),
                jnp.concatenate([imag_t, -real_t], axis=1),
            ]
        ):
            upper = jnp.dot(left[:half], right, preferred_element_type=jnp.float32) * scale
            corner = upper[:, half:].T
            out_ref[chan, kind, 0:half, :] = upper
            out_ref[chan, kind, half:, 0:half] = -corner if kind else corner
            out_ref[chan, kind, half:, half:] = (
                jnp.dot(left[half:], right[:, half:], preferred_element_type=jnp.float32) * scale
            )


def correlate(arrived, n_inp):
    sources, rows, frames, inputs = arrived.shape
    count = rows // 2
    inputs_all = n_inp * inputs
    frames_all = sources // n_inp * frames
    return pl.pallas_call(
        functools.partial(correlate_kernel, n_inp, 1.0 / frames_all),
        grid=(count // 2,),
        out_shape=jax.ShapeDtypeStruct((count, 2, inputs_all, inputs_all), jnp.float32),
        in_specs=[pl.BlockSpec((sources, 4, frames, inputs), lambda c: (0, c, 0, 0))],
        out_specs=pl.BlockSpec((2, 2, inputs_all, inputs_all), lambda c: (c, 0, 0, 0)),
        compiler_params=pltpu.CompilerParams(vmem_limit_bytes=48 * 1024 * 1024),
        cost_estimate=pl.CostEstimate(
            flops=count * 8 * inputs_all * inputs_all * frames_all,
            bytes_accessed=arrived.size * 2 + count * 8 * inputs_all * inputs_all,
            transcendentals=0,
        ),
        name="correlate",
    )(arrived)


def on_device(samples, eq_gain):
    local_inputs, local_frames, nfft = samples.shape
    n_inp = lax.axis_size("inp")
    n_time = lax.axis_size("tm")
    if local_inputs != LANES or n_inp != 4 or n_time != 8 or local_frames % STEP or local_frames < 2 * STEP:
        return plain_plan(samples, eq_gain)
    arrived = spread(samples, eq_gain, n_inp, n_time)
    return correlate(arrived, n_inp)


def solution(mesh):
    placed = (P("inp", "tm", None), P(None, "inp"))
    return jax.shard_map(
        on_device,
        mesh=mesh,
        in_specs=placed,
        out_specs=P(("inp", "tm"), None, None, None),
        check_vma=False,
    )
```

```python
import functools
import math

import jax
import jax.numpy as jnp
import numpy as np
from jax import lax
from jax.experimental import pallas as pl
from jax.experimental.pallas import tpu as pltpu
from jax.sharding import PartitionSpec as P

TAPS = 4
LANES = 128
STEP = 16


def passed_along(array, axis, by):
    devices = lax.axis_size(axis)
    pairs = [(i, i + by) for i in range(devices) if 0 <= i + by < devices]
    return lax.ppermute(array, axis, pairs)


def window_table(taps, nfft):
    position = np.arange(taps * nfft, dtype=np.float64) + 0.5
    shape_part = np.sinc(position / nfft - taps / 2.0)
    taper = 0.5 - 0.5 * np.cos(position * (2.0 * math.pi / (taps * nfft)))
    return (shape_part * taper).reshape(taps, nfft).astype(np.float32)


def fourier_table(channels, nfft):
    chan = np.arange(channels)
    point = np.arange(nfft)
    phase = (chan[:, None] * point[None, :] % nfft) * (2.0 * math.pi / nfft)
    scale = 1.0 / math.sqrt(nfft)
    table = np.stack([np.cos(phase) * scale, -np.sin(phase) * scale], axis=1)
    return table.reshape(2 * channels, nfft).astype(np.float32).astype(jnp.bfloat16)


def correlate_einsum(blocks, frames_all):
    groups_in = blocks.shape[0]
    count = blocks.shape[2]
    local_inputs = blocks.shape[4]
    inputs_all = groups_in * local_inputs
    gram = jnp.einsum("ptcraf,qtcsbf->crpasqb", blocks, blocks, preferred_element_type=jnp.float32)
    gram = gram.reshape(count, 2, inputs_all, 2, inputs_all)
    real_part = (gram[:, 0, :, 0, :] + gram[:, 1, :, 1, :]) / frames_all
    imag_part = (gram[:, 1, :, 0, :] - gram[:, 0, :, 1, :]) / frames_all
    return jnp.stack([real_part, imag_part], axis=1)


def plain_plan(samples, eq_gain):
    local_inputs, local_frames, nfft = samples.shape
    channels = nfft // 2
    n_inp = lax.axis_size("inp")
    n_time = lax.axis_size("tm")
    groups = n_inp * n_time
    chan_dev = channels // groups
    frames_all = n_time * local_frames
    tail = samples[:, local_frames - (TAPS - 1) :, :]
    before = passed_along(tail, "tm", 1)
    padded = jnp.concatenate([before, samples], axis=1)
    window = window_table(TAPS, nfft)
    filtered = jnp.zeros((local_inputs, local_frames, nfft), jnp.float32)
    for tap in range(TAPS):
        filtered = filtered + window[tap] * padded[:, tap : tap + local_frames, :].astype(
            jnp.float32
        )
    filtered = filtered.astype(jnp.bfloat16)
    table = jnp.asarray(fourier_table(channels, nfft))
    spectra = lax.dot_general(
        table, filtered, (((1,), (2,)), ((), ())), preferred_element_type=jnp.float32
    )
    spectra = spectra.reshape(channels, 2, local_inputs, local_frames) * eq_gain[:, None, :, None]
    spectra = spectra.astype(jnp.bfloat16)
    parcel = spectra.reshape(1, groups, chan_dev, 2, local_inputs, local_frames)
    arrived = lax.all_to_all(parcel, ("inp", "tm"), split_axis=1, concat_axis=0, tiled=True)
    count = arrived.shape[2]
    blocks = arrived.reshape(n_inp, n_time, count, 2, local_inputs, local_frames)
    return correlate_einsum(blocks, frames_all)


def spread_kernel(
    n_inp, n_time,
    x_hbm, gain_ref, table_ref, window_ref,
    recv_hbm, late_hbm,
    xbuf, turned, tail, taps_buf, halo_out, halo_in, filt, freq, send,
    load_sem, send_sem, recv_sem, halo_send_sem, halo_recv_sem, own_sem, late_sem,
):
    groups = n_inp * n_time
    inputs, frames, nfft = x_hbm.shape
    rows_all = table_ref.shape[0]
    rows_plane = rows_all // n_inp
    rows_dev = rows_all // groups
    pitch = freq.shape[0] // STEP
    steps = frames // STEP
    tiles = nfft // LANES
    keep = TAPS - 1
    z = lax.axis_index("inp")
    t = lax.axis_index("tm")
    me = z * n_time + t

    def load(step):
        f0 = pl.multiple_of(step * STEP, STEP)
        slot = lax.rem(step, 2)
        return pltpu.make_async_copy(
            x_hbm.at[:, pl.ds(f0, STEP), :], xbuf.at[slot], load_sem.at[slot]
        )

    load(steps - 1).start()
    load(steps - 2).start()
    barrier = pltpu.get_barrier_semaphore()

    @pl.loop(1, groups)
    def _(s):
        d = lax.rem(me + s, groups)
        pl.semaphore_signal(
            barrier, inc=1, device_id=(d // n_time, lax.rem(d, n_time)),
            device_id_type=pl.DeviceIdType.MESH,
        )

    rows_first = rows_dev // 2

    def send_one(step, d_z, s, count=rows_dev):
        d_t = lax.rem(t + s, n_time)
        f0 = pl.multiple_of(step * STEP, STEP)
        d = d_z * n_time + d_t
        r0 = pl.multiple_of(d * rows_dev, rows_dev)
        pltpu.make_async_remote_copy(
            src_ref=send.at[pl.ds(r0, count), pl.ds(f0, STEP), :],
            dst_ref=recv_hbm.at[me, pl.ds(0, count), pl.ds(f0, STEP), :],
            send_sem=send_sem.at[d],
            recv_sem=recv_sem.at[me],
            device_id=(d_z, d_t),
            device_id_type=pl.DeviceIdType.MESH,
        ).start()

    def halo():
        return pltpu.make_async_remote_copy(
            src_ref=halo_out,
            dst_ref=halo_in,
            send_sem=halo_send_sem,
            recv_sem=halo_recv_sem,
            device_id=(z, lax.rem(t + 1, n_time)),
            device_id_type=pl.DeviceIdType.MESH,
        )

    def filter_step(step):
        slot = lax.rem(step, 2)

        @pl.loop(0, tiles)
        def _(tile):
            lanes = pl.ds(pl.multiple_of(tile * LANES, LANES), LANES)
            turned[...] = (
                xbuf[slot, :, :, lanes].astype(jnp.float32).reshape(inputs * STEP, LANES)
            )

            @pl.when(step > 0)
            def _():
                earlier = xbuf[1 - slot, :, :, lanes].astype(jnp.float32)[:, STEP - 8 :, :]
                tail[...] = earlier.reshape(inputs * 8, LANES)
                for k in range(keep):
                    taps_buf[k] = tail[pl.ds(8 - keep + k, inputs, stride=8), :]

            @pl.when(step == 0)
            def _():
                taps_buf[0:keep] = halo_in[:, :, lanes].astype(jnp.float32)

            for f in range(STEP):
                taps_buf[keep + f] = turned[pl.ds(f, inputs, stride=STEP), :]

            @pl.when(step == steps - 1)
            def _():
                halo_out[:, :, lanes] = taps_buf[STEP : STEP + keep].astype(jnp.bfloat16)

            for f in range(STEP):
                total = window_ref[0:1, lanes] * taps_buf[f]
                for tap in range(1, TAPS):
                    total = total + window_ref[tap : tap + 1, lanes] * taps_buf[f + tap]
                filt[f * inputs : (f + 1) * inputs, lanes] = total.astype(jnp.bfloat16)

    def transform(step, plane):
        f0 = pl.multiple_of(step * STEP, STEP)
        base = pl.multiple_of(plane * rows_plane, rows_plane)
        width = 4

        @pl.loop(0, STEP // width)
        def _(j):
            some = filt[pl.ds(pl.multiple_of(j * width * inputs, width * inputs), width * inputs), :]
            got = lax.dot_general(
                table_ref[pl.ds(base, rows_plane), :], some,
                (((1,), (1,)), ((), ())), preferred_element_type=jnp.float32,
            )
            for w in range(width):
                at = pl.multiple_of((j * width + w) * pitch, 8)
                freq[pl.ds(at, rows_plane), :] = got[:, w * inputs : (w + 1) * inputs]

        @pl.loop(0, rows_plane // 8)
        def _(i):
            for k in range(8):
                row = i * 8 + k
                chan = plane * (rows_plane // 2) + i * 4 + k // 2
                value = freq[pl.ds(row, STEP, stride=pitch), :] * gain_ref[pl.ds(chan, 1), :]
                send[base + row, pl.ds(f0, STEP), :] = value.astype(jnp.bfloat16)

    far = lax.rem(z + 2, 4)
    farther = 3 - z
    near = z + 1 - 2 * lax.rem(z, 2)
    half = n_time // 2

    @pl.loop(0, steps)
    def _(turn):
        step = steps - 1 - turn

        @pl.when(turn == 0)
        def _():
            load(steps - 1).wait()

        @pl.when(step > 0)
        def _():
            load(step - 1).wait()

        @pl.when(step == 0)
        def _():
            @pl.when(t > 0)
            def _():
                halo().wait_recv()

            @pl.when(t == 0)
            def _():
                halo_in[...] = jnp.zeros_like(halo_in)

        filter_step(step)

        @pl.when(step > 1)
        def _():
            load(step - 2).start()

        transform(step, far)

        @pl.when(turn == 0)
        def _():
            pl.semaphore_wait(barrier, groups - 1)

            @pl.when(t < n_time - 1)
            def _():
                halo().start()

        send_one(step, far, 0, rows_first)

        @pl.loop(1, half)
        def _(s):
            send_one(step, far, s)

        transform(step, z)

        @pl.loop(0, half)
        def _(s):
            send_one(step, far, s + half)
            send_one(step, z, s + half)

            @pl.when(s > 0)
            def _():
                send_one(step, z, s)

        transform(step, near)
        transform(step, farther)

        @pl.loop(0, n_time)
        def _(s):
            send_one(step, near, s)
            send_one(step, farther, s)

    own = pltpu.make_async_copy(
        send.at[pl.ds(pl.multiple_of(me * rows_dev, rows_dev), rows_dev)], recv_hbm.at[me], own_sem
    )
    own.start()
    partner = far * n_time + t
    late_row = pl.multiple_of(partner * rows_dev + rows_first, rows_first)
    late = pltpu.make_async_copy(send.at[pl.ds(late_row, rows_first)], late_hbm, late_sem)
    late.start()
    own.wait()
    late.wait()

    @pl.when(t < n_time - 1)
    def _():
        halo().wait_send()

    def finish(d, count):
        gone = send.at[pl.ds(pl.multiple_of(d * rows_dev, rows_dev), count)]
        pltpu.make_async_copy(gone, gone, send_sem.at[d]).wait()
        here = recv_hbm.at[d, pl.ds(0, count)]
        pltpu.make_async_copy(here, here, recv_sem.at[d]).wait()

    @pl.loop(1, groups)
    def _(s):
        d = lax.rem(me + s, groups)

        @pl.when(d == partner)
        def _():
            finish(d, rows_first)

        @pl.when(d != partner)
        def _():
            finish(d, rows_dev)


def spread(samples, eq_gain, n_inp, n_time):
    inputs, frames, nfft = samples.shape
    channels = nfft // 2
    rows = 2 * channels
    groups = n_inp * n_time
    pitch = rows // n_inp + 8
    vmem = pl.BlockSpec(memory_space=pltpu.VMEM)
    anywhere = pl.BlockSpec(memory_space=pl.ANY)
    return pl.pallas_call(
        functools.partial(spread_kernel, n_inp, n_time),
        out_shape=[
            jax.ShapeDtypeStruct((groups, rows // groups, frames, inputs), jnp.bfloat16),
            jax.ShapeDtypeStruct((rows // groups // 2, frames, inputs), jnp.bfloat16),
        ],
        in_specs=[anywhere, vmem, vmem, vmem],
        out_specs=[anywhere, anywhere],
        scratch_shapes=[
            pltpu.VMEM((2, inputs, STEP, nfft), jnp.bfloat16),
            pltpu.VMEM((inputs * STEP, LANES), jnp.float32),
            pltpu.VMEM((inputs * 8, LANES), jnp.float32),
            pltpu.VMEM((STEP + TAPS - 1, inputs, LANES), jnp.float32),
            pltpu.VMEM((TAPS - 1, inputs, nfft), jnp.bfloat16),
            pltpu.VMEM((TAPS - 1, inputs, nfft), jnp.bfloat16),
            pltpu.VMEM((STEP * inputs, nfft), jnp.bfloat16),
            pltpu.VMEM((STEP * pitch, LANES), jnp.float32),
            pltpu.VMEM((rows, frames, inputs), jnp.bfloat16),
            pltpu.SemaphoreType.DMA((2,)),
            pltpu.SemaphoreType.DMA((groups,)),
            pltpu.SemaphoreType.DMA((groups,)),
            pltpu.SemaphoreType.DMA,
            pltpu.SemaphoreType.DMA,
            pltpu.SemaphoreType.DMA,
            pltpu.SemaphoreType.DMA,
        ],
        compiler_params=pltpu.CompilerParams(
            collective_id=0, has_side_effects=True, vmem_limit_bytes=56 * 1024 * 1024
        ),
        cost_estimate=pl.CostEstimate(
            flops=2 * rows * nfft * inputs * frames,
            bytes_accessed=4 * inputs * frames * nfft,
            transcendentals=0,
        ),
        name="filter_transform_spread",
    )(
        samples, eq_gain,
        jnp.asarray(fourier_table(channels, nfft)), jnp.asarray(window_table(TAPS, nfft)),
    )


def correlate_kernel(n_inp, scale, block_ref, *refs):
    late_ref = refs[0] if len(refs) > 1 else None
    out_ref = refs[-1]
    sources, rows, frames, inputs = block_ref.shape
    n_time = sources // n_inp
    half = n_inp * inputs // 2
    if late_ref is not None:
        partner = lax.rem(lax.axis_index("inp") + 2, 4) * n_time + lax.axis_index("tm")

    def from_source(src, row):
        if late_ref is None:
            return block_ref[src, row]
        return jnp.where(partner == src, late_ref[row], block_ref[src, row])

    def part(row):
        pieces = [
            jnp.concatenate([from_source(p * n_time + q, row) for q in range(n_time)], axis=0)
            for p in range(n_inp)
        ]
        return jnp.concatenate(pieces, axis=1)

    for chan in range(rows // 2):
        real, imag = part(2 * chan), part(2 * chan + 1)
        real_t, imag_t = real.T, imag.T
        right = jnp.concatenate([real, imag], axis=0)
        for kind, left in enumerate(
            [
                jnp.concatenate([real_t, imag_t], axis=1),
                jnp.concatenate([imag_t, -real_t], axis=1),
            ]
        ):
            upper = jnp.dot(left[:half], right, preferred_element_type=jnp.float32) * scale
            corner = upper[:, half:].T
            out_ref[chan, kind, 0:half, :] = upper
            out_ref[chan, kind, half:, 0:half] = -corner if kind else corner
            out_ref[chan, kind, half:, half:] = (
                jnp.dot(left[half:], right[:, half:], preferred_element_type=jnp.float32) * scale
            )


def correlate(arrived, n_inp, late=None, before=None):
    sources, rows, frames, inputs = arrived.shape
    count = rows // 2
    inputs_all = n_inp * inputs
    frames_all = sources // n_inp * frames
    turns = count // 4
    first = 0 if before is None else turns
    in_specs = [pl.BlockSpec((sources, 4, frames, inputs), lambda c: (0, c + first, 0, 0))]
    operands = [arrived]
    aliases = {}
    body = functools.partial(correlate_kernel, n_inp, 1.0 / frames_all)
    if before is not None:
        in_specs.append(pl.BlockSpec((4, frames, inputs), lambda c: (c, 0, 0)))
        in_specs.append(pl.BlockSpec(memory_space=pl.ANY))
        operands += [late, before]
        aliases = {2: 0}
        whole = body
        body = lambda block_ref, late_ref, _, out_ref: whole(block_ref, late_ref, out_ref)
    return pl.pallas_call(
        body,
        grid=(turns,),
        out_shape=jax.ShapeDtypeStruct((count, 2, inputs_all, inputs_all), jnp.float32),
        in_specs=in_specs,
        out_specs=pl.BlockSpec((2, 2, inputs_all, inputs_all), lambda c: (c + first, 0, 0, 0)),
        input_output_aliases=aliases,
        compiler_params=pltpu.CompilerParams(vmem_limit_bytes=48 * 1024 * 1024),
        cost_estimate=pl.CostEstimate(
            flops=count * 3 * inputs_all * inputs_all * frames_all,
            bytes_accessed=arrived.size + count * 4 * inputs_all * inputs_all,
            transcendentals=0,
        ),
        name="correlate_first" if before is None else "correlate_second",
    )(*operands)


def on_device(samples, eq_gain):
    local_inputs, local_frames, nfft = samples.shape
    n_inp = lax.axis_size("inp")
    n_time = lax.axis_size("tm")
    if local_inputs != LANES or n_inp != 4 or n_time != 8 or local_frames % STEP or local_frames < 2 * STEP:
        return plain_plan(samples, eq_gain)
    arrived, late = spread(samples, eq_gain, n_inp, n_time)
    late = lax.ppermute(late, "inp", [(i, (i + 2) % n_inp) for i in range(n_inp)])
    first = correlate(arrived, n_inp)
    return correlate(arrived, n_inp, late, first)


def solution(mesh):
    placed = (P("inp", "tm", None), P(None, "inp"))
    return jax.shard_map(
        on_device,
        mesh=mesh,
        in_specs=placed,
        out_specs=P(("inp", "tm"), None, None, None),
        check_vma=False,
    )
```

```python
import functools
import math

import jax
import jax.numpy as jnp
import numpy as np
from jax import lax
from jax.experimental import pallas as pl
from jax.experimental.pallas import tpu as pltpu
from jax.sharding import PartitionSpec as P

TAPS = 4
LANES = 128
STEP = 16


def passed_along(array, axis, by):
    devices = lax.axis_size(axis)
    pairs = [(i, i + by) for i in range(devices) if 0 <= i + by < devices]
    return lax.ppermute(array, axis, pairs)


def window_table(taps, nfft):
    position = np.arange(taps * nfft, dtype=np.float64) + 0.5
    shape_part = np.sinc(position / nfft - taps / 2.0)
    taper = 0.5 - 0.5 * np.cos(position * (2.0 * math.pi / (taps * nfft)))
    return (shape_part * taper).reshape(taps, nfft).astype(np.float32)


def fourier_table(channels, nfft):
    chan = np.arange(channels)
    point = np.arange(nfft)
    phase = (chan[:, None] * point[None, :] % nfft) * (2.0 * math.pi / nfft)
    scale = 1.0 / math.sqrt(nfft)
    table = np.stack([np.cos(phase) * scale, -np.sin(phase) * scale], axis=1)
    return table.reshape(2 * channels, nfft).astype(np.float32).astype(jnp.bfloat16)


def correlate_einsum(blocks, frames_all):
    groups_in = blocks.shape[0]
    count = blocks.shape[2]
    local_inputs = blocks.shape[4]
    inputs_all = groups_in * local_inputs
    gram = jnp.einsum("ptcraf,qtcsbf->crpasqb", blocks, blocks, preferred_element_type=jnp.float32)
    gram = gram.reshape(count, 2, inputs_all, 2, inputs_all)
    real_part = (gram[:, 0, :, 0, :] + gram[:, 1, :, 1, :]) / frames_all
    imag_part = (gram[:, 1, :, 0, :] - gram[:, 0, :, 1, :]) / frames_all
    return jnp.stack([real_part, imag_part], axis=1)


def plain_plan(samples, eq_gain):
    local_inputs, local_frames, nfft = samples.shape
    channels = nfft // 2
    n_inp = lax.axis_size("inp")
    n_time = lax.axis_size("tm")
    groups = n_inp * n_time
    chan_dev = channels // groups
    frames_all = n_time * local_frames
    tail = samples[:, local_frames - (TAPS - 1) :, :]
    before = passed_along(tail, "tm", 1)
    padded = jnp.concatenate([before, samples], axis=1)
    window = window_table(TAPS, nfft)
    filtered = jnp.zeros((local_inputs, local_frames, nfft), jnp.float32)
    for tap in range(TAPS):
        filtered = filtered + window[tap] * padded[:, tap : tap + local_frames, :].astype(
            jnp.float32
        )
    filtered = filtered.astype(jnp.bfloat16)
    table = jnp.asarray(fourier_table(channels, nfft))
    spectra = lax.dot_general(
        table, filtered, (((1,), (2,)), ((), ())), preferred_element_type=jnp.float32
    )
    spectra = spectra.reshape(channels, 2, local_inputs, local_frames) * eq_gain[:, None, :, None]
    spectra = spectra.astype(jnp.bfloat16)
    parcel = spectra.reshape(1, groups, chan_dev, 2, local_inputs, local_frames)
    arrived = lax.all_to_all(parcel, ("inp", "tm"), split_axis=1, concat_axis=0, tiled=True)
    count = arrived.shape[2]
    blocks = arrived.reshape(n_inp, n_time, count, 2, local_inputs, local_frames)
    return correlate_einsum(blocks, frames_all)


def spread_kernel(
    n_inp, n_time,
    x_hbm, gain_ref, table_ref, window_ref,
    recv_hbm, late_far_hbm, late_farther_hbm,
    xbuf, turned, tail, taps_buf, halo_out, halo_in, filt, freq, send,
    load_sem, send_sem, recv_sem, halo_send_sem, halo_recv_sem, own_sem, late_sem,
):
    groups = n_inp * n_time
    inputs, frames, nfft = x_hbm.shape
    rows_all = table_ref.shape[0]
    rows_plane = rows_all // n_inp
    rows_dev = rows_all // groups
    pitch = freq.shape[0] // STEP
    steps = frames // STEP
    tiles = nfft // LANES
    keep = TAPS - 1
    z = lax.axis_index("inp")
    t = lax.axis_index("tm")
    me = z * n_time + t

    def load(step):
        f0 = pl.multiple_of(step * STEP, STEP)
        slot = lax.rem(step, 2)
        return pltpu.make_async_copy(
            x_hbm.at[:, pl.ds(f0, STEP), :], xbuf.at[slot], load_sem.at[slot]
        )

    load(steps - 1).start()
    load(steps - 2).start()
    barrier = pltpu.get_barrier_semaphore()

    @pl.loop(1, groups)
    def _(s):
        d = lax.rem(me + s, groups)
        pl.semaphore_signal(
            barrier, inc=1, device_id=(d // n_time, lax.rem(d, n_time)),
            device_id_type=pl.DeviceIdType.MESH,
        )

    rows_late = late_far_hbm.shape[0]
    rows_first = rows_dev - rows_late

    def send_one(step, d_z, s, count=rows_dev):
        d_t = lax.rem(t + s, n_time)
        f0 = pl.multiple_of(step * STEP, STEP)
        d = d_z * n_time + d_t
        r0 = pl.multiple_of(d * rows_dev, rows_dev)
        pltpu.make_async_remote_copy(
            src_ref=send.at[pl.ds(r0, count), pl.ds(f0, STEP), :],
            dst_ref=recv_hbm.at[me, pl.ds(0, count), pl.ds(f0, STEP), :],
            send_sem=send_sem.at[d],
            recv_sem=recv_sem.at[me],
            device_id=(d_z, d_t),
            device_id_type=pl.DeviceIdType.MESH,
        ).start()

    def halo():
        return pltpu.make_async_remote_copy(
            src_ref=halo_out,
            dst_ref=halo_in,
            send_sem=halo_send_sem,
            recv_sem=halo_recv_sem,
            device_id=(z, lax.rem(t + 1, n_time)),
            device_id_type=pl.DeviceIdType.MESH,
        )

    def filter_step(step):
        slot = lax.rem(step, 2)

        @pl.loop(0, tiles)
        def _(tile):
            lanes = pl.ds(pl.multiple_of(tile * LANES, LANES), LANES)
            turned[...] = (
                xbuf[slot, :, :, lanes].astype(jnp.float32).reshape(inputs * STEP, LANES)
            )

            @pl.when(step > 0)
            def _():
                earlier = xbuf[1 - slot, :, :, lanes].astype(jnp.float32)[:, STEP - 8 :, :]
                tail[...] = earlier.reshape(inputs * 8, LANES)
                for k in range(keep):
                    taps_buf[k] = tail[pl.ds(8 - keep + k, inputs, stride=8), :]

            @pl.when(step == 0)
            def _():
                taps_buf[...] = halo_in[:, :, lanes].astype(jnp.float32)

            @pl.when(step == steps - 1)
            def _():
                for k in range(keep):
                    last = turned[pl.ds(STEP - keep + k, inputs, stride=STEP), :]
                    halo_out[k, :, lanes] = last.astype(jnp.bfloat16)

            some = 32
            weights = [
                jnp.broadcast_to(window_ref[tap : tap + 1, lanes], (some, LANES))
                for tap in range(TAPS)
            ]
            for i0 in range(0, inputs, some):
                held = [taps_buf[k, i0 : i0 + some] for k in range(keep)]
                for f in range(STEP):
                    held.append(turned[pl.ds(i0 * STEP + f, some, stride=STEP), :])
                    total = weights[0] * held[0]
                    for tap in range(1, TAPS):
                        total = total + weights[tap] * held[tap]
                    filt[f * inputs + i0 : f * inputs + i0 + some, lanes] = total.astype(
                        jnp.bfloat16
                    )
                    held.pop(0)

    def transform(step, plane):
        f0 = pl.multiple_of(step * STEP, STEP)
        base = pl.multiple_of(plane * rows_plane, rows_plane)
        width = 4

        @pl.loop(0, STEP // width)
        def _(j):
            some = filt[pl.ds(pl.multiple_of(j * width * inputs, width * inputs), width * inputs), :]
            got = lax.dot_general(
                table_ref[pl.ds(base, rows_plane), :], some,
                (((1,), (1,)), ((), ())), preferred_element_type=jnp.float32,
            )
            for w in range(width):
                at = pl.multiple_of((j * width + w) * pitch, 8)
                freq[pl.ds(at, rows_plane), :] = got[:, w * inputs : (w + 1) * inputs]

        @pl.loop(0, rows_plane // 8)
        def _(i):
            for k in range(8):
                row = i * 8 + k
                chan = plane * (rows_plane // 2) + i * 4 + k // 2
                value = freq[pl.ds(row, STEP, stride=pitch), :] * gain_ref[pl.ds(chan, 1), :]
                send[base + row, pl.ds(f0, STEP), :] = value.astype(jnp.bfloat16)

    far = lax.rem(z + 2, 4)
    farther = 3 - z
    near = z + 1 - 2 * lax.rem(z, 2)
    half = n_time // 2

    @pl.loop(0, steps)
    def _(turn):
        step = steps - 1 - turn

        @pl.when(turn == 0)
        def _():
            load(steps - 1).wait()

        @pl.when(step > 0)
        def _():
            load(step - 1).wait()

        @pl.when(step == 0)
        def _():
            @pl.when(t > 0)
            def _():
                halo().wait_recv()

            @pl.when(t == 0)
            def _():
                halo_in[...] = jnp.zeros_like(halo_in)

        filter_step(step)

        @pl.when(step > 1)
        def _():
            load(step - 2).start()

        transform(step, far)

        @pl.when(turn == 0)
        def _():
            pl.semaphore_wait(barrier, groups - 1)

            @pl.when(t < n_time - 1)
            def _():
                halo().start()

        send_one(step, far, 0, rows_first)

        @pl.loop(1, half)
        def _(s):
            send_one(step, far, s)

        transform(step, z)

        @pl.loop(0, half)
        def _(s):
            send_one(step, far, s + half)
            send_one(step, z, s + half)

            @pl.when(s > 0)
            def _():
                send_one(step, z, s)

        transform(step, near)
        transform(step, farther)

        send_one(step, near, 0)
        send_one(step, farther, 0, rows_first)

        @pl.loop(1, n_time)
        def _(s):
            send_one(step, near, s)
            send_one(step, farther, s)

    own = pltpu.make_async_copy(
        send.at[pl.ds(pl.multiple_of(me * rows_dev, rows_dev), rows_dev)], recv_hbm.at[me], own_sem
    )
    own.start()
    partners = (far * n_time + t, farther * n_time + t)
    late = [
        pltpu.make_async_copy(
            send.at[pl.ds(partner * rows_dev + rows_first, rows_late)], late_hbm, late_sem.at[k]
        )
        for k, (partner, late_hbm) in enumerate(zip(partners, (late_far_hbm, late_farther_hbm)))
    ]
    for copy in late:
        copy.start()
    own.wait()
    for copy in late:
        copy.wait()

    @pl.when(t < n_time - 1)
    def _():
        halo().wait_send()

    def finish(d, count):
        gone = send.at[pl.ds(pl.multiple_of(d * rows_dev, rows_dev), count)]
        pltpu.make_async_copy(gone, gone, send_sem.at[d]).wait()
        here = recv_hbm.at[d, pl.ds(0, count)]
        pltpu.make_async_copy(here, here, recv_sem.at[d]).wait()

    @pl.loop(1, groups)
    def _(s):
        d = lax.rem(me + s, groups)

        @pl.when((d == partners[0]) | (d == partners[1]))
        def _():
            finish(d, rows_first)

        @pl.when((d != partners[0]) & (d != partners[1]))
        def _():
            finish(d, rows_dev)


def spread(samples, eq_gain, n_inp, n_time, late):
    inputs, frames, nfft = samples.shape
    channels = nfft // 2
    rows = 2 * channels
    groups = n_inp * n_time
    pitch = rows // n_inp + 8
    vmem = pl.BlockSpec(memory_space=pltpu.VMEM)
    anywhere = pl.BlockSpec(memory_space=pl.ANY)
    return pl.pallas_call(
        functools.partial(spread_kernel, n_inp, n_time),
        out_shape=[
            jax.ShapeDtypeStruct((groups, rows // groups, frames, inputs), jnp.bfloat16),
            jax.ShapeDtypeStruct((2 * late, frames, inputs), jnp.bfloat16),
            jax.ShapeDtypeStruct((2 * late, frames, inputs), jnp.bfloat16),
        ],
        in_specs=[anywhere, vmem, vmem, vmem],
        out_specs=[anywhere] * 3,
        scratch_shapes=[
            pltpu.VMEM((2, inputs, STEP, nfft), jnp.bfloat16),
            pltpu.VMEM((inputs * STEP, LANES), jnp.float32),
            pltpu.VMEM((inputs * 8, LANES), jnp.float32),
            pltpu.VMEM((TAPS - 1, inputs, LANES), jnp.float32),
            pltpu.VMEM((TAPS - 1, inputs, nfft), jnp.bfloat16),
            pltpu.VMEM((TAPS - 1, inputs, nfft), jnp.bfloat16),
            pltpu.VMEM((STEP * inputs, nfft), jnp.bfloat16),
            pltpu.VMEM((STEP * pitch, LANES), jnp.float32),
            pltpu.VMEM((rows, frames, inputs), jnp.bfloat16),
            pltpu.SemaphoreType.DMA((2,)),
            pltpu.SemaphoreType.DMA((groups,)),
            pltpu.SemaphoreType.DMA((groups,)),
            pltpu.SemaphoreType.DMA,
            pltpu.SemaphoreType.DMA,
            pltpu.SemaphoreType.DMA,
            pltpu.SemaphoreType.DMA((2,)),
        ],
        compiler_params=pltpu.CompilerParams(
            collective_id=0, has_side_effects=True, vmem_limit_bytes=56 * 1024 * 1024
        ),
        cost_estimate=pl.CostEstimate(
            flops=2 * rows * nfft * inputs * frames,
            bytes_accessed=4 * inputs * frames * nfft,
            transcendentals=0,
        ),
        name="filter_transform_spread",
    )(
        samples, eq_gain,
        jnp.asarray(fourier_table(channels, nfft)), jnp.asarray(window_table(TAPS, nfft)),
    )


def correlate_kernel(n_inp, scale, block_ref, *refs):
    late_refs = refs[:-1]
    out_ref = refs[-1]
    sources, rows, frames, inputs = block_ref.shape
    n_time = sources // n_inp
    half = n_inp * inputs // 2
    if late_refs:
        z, t = lax.axis_index("inp"), lax.axis_index("tm")
        partners = (lax.rem(z + 2, 4) * n_time + t, (3 - z) * n_time + t)

    def from_source(src, row):
        value = block_ref[src, row]
        if late_refs:
            for partner, late_ref in zip(partners, late_refs):
                value = jnp.where(partner == src, late_ref[row], value)
        return value

    def part(row):
        pieces = [
            jnp.concatenate([from_source(p * n_time + q, row) for q in range(n_time)], axis=0)
            for p in range(n_inp)
        ]
        return jnp.concatenate(pieces, axis=1)

    for chan in range(rows // 2):
        real, imag = part(2 * chan), part(2 * chan + 1)
        real_t, imag_t = real.T, imag.T
        right = jnp.concatenate([real, imag], axis=0)
        for kind, left in enumerate(
            [
                jnp.concatenate([real_t, imag_t], axis=1),
                jnp.concatenate([imag_t, -real_t], axis=1),
            ]
        ):
            upper = jnp.dot(left[:half], right, preferred_element_type=jnp.float32) * scale
            corner = upper[:, half:].T
            out_ref[chan, kind, 0:half, :] = upper
            out_ref[chan, kind, half:, 0:half] = -corner if kind else corner
            out_ref[chan, kind, half:, half:] = (
                jnp.dot(left[half:], right[:, half:], preferred_element_type=jnp.float32) * scale
            )


def correlate(arrived, n_inp, late_chans, late=(), before=None):
    sources, rows, frames, inputs = arrived.shape
    count = rows // 2
    inputs_all = n_inp * inputs
    frames_all = sources // n_inp * frames
    turns = (count - late_chans if before is None else late_chans) // 2
    first = 0 if before is None else (count - late_chans) // 2
    in_specs = [pl.BlockSpec((sources, 4, frames, inputs), lambda c: (0, c + first, 0, 0))]
    operands = [arrived]
    aliases = {}
    body = functools.partial(correlate_kernel, n_inp, 1.0 / frames_all)
    if before is not None:
        in_specs += [pl.BlockSpec((4, frames, inputs), lambda c: (c, 0, 0)) for _ in late]
        in_specs.append(pl.BlockSpec(memory_space=pl.ANY))
        operands += [*late, before]
        aliases = {len(operands) - 1: 0}
        whole = body
        body = lambda *refs: whole(*refs[:-2], refs[-1])
    return pl.pallas_call(
        body,
        grid=(turns,),
        out_shape=jax.ShapeDtypeStruct((count, 2, inputs_all, inputs_all), jnp.float32),
        in_specs=in_specs,
        out_specs=pl.BlockSpec((2, 2, inputs_all, inputs_all), lambda c: (c + first, 0, 0, 0)),
        input_output_aliases=aliases,
        compiler_params=pltpu.CompilerParams(vmem_limit_bytes=48 * 1024 * 1024),
        cost_estimate=pl.CostEstimate(
            flops=turns * 12 * inputs_all * inputs_all * frames_all,
            bytes_accessed=turns * (4 * arrived.size // count + 16 * inputs_all * inputs_all),
            transcendentals=0,
        ),
        name="correlate_first" if before is None else "correlate_second",
    )(*operands)


def on_device(samples, eq_gain):
    local_inputs, local_frames, nfft = samples.shape
    n_inp = lax.axis_size("inp")
    n_time = lax.axis_size("tm")
    if local_inputs != LANES or n_inp != 4 or n_time != 8 or local_frames % STEP or local_frames < 2 * STEP or nfft != 1024:
        return plain_plan(samples, eq_gain)
    late_chans = nfft // 2 // (n_inp * n_time) * 3 // 8
    arrived, far, farther = spread(samples, eq_gain, n_inp, n_time, late_chans)
    far = lax.ppermute(far, "inp", [(i, (i + 2) % n_inp) for i in range(n_inp)])
    farther = lax.ppermute(farther, "inp", [(i, n_inp - 1 - i) for i in range(n_inp)])
    first = correlate(arrived, n_inp, late_chans)
    return correlate(arrived, n_inp, late_chans, (far, farther), first)


def solution(mesh):
    placed = (P("inp", "tm", None), P(None, "inp"))
    return jax.shard_map(
        on_device,
        mesh=mesh,
        in_specs=placed,
        out_specs=P(("inp", "tm"), None, None, None),
        check_vma=False,
    )
```

```python
import functools
import math

import jax
import jax.numpy as jnp
import numpy as np
from jax import lax
from jax.experimental import pallas as pl
from jax.experimental.pallas import tpu as pltpu
from jax.sharding import PartitionSpec as P

TAPS = 4
LANES = 128
STEP = 16


def passed_along(array, axis, by):
    devices = lax.axis_size(axis)
    pairs = [(i, i + by) for i in range(devices) if 0 <= i + by < devices]
    return lax.ppermute(array, axis, pairs)


def window_table(taps, nfft):
    position = np.arange(taps * nfft, dtype=np.float64) + 0.5
    shape_part = np.sinc(position / nfft - taps / 2.0)
    taper = 0.5 - 0.5 * np.cos(position * (2.0 * math.pi / (taps * nfft)))
    return (shape_part * taper).reshape(taps, nfft).astype(np.float32)


def fourier_table(channels, nfft):
    chan = np.arange(channels)
    point = np.arange(nfft)
    phase = (chan[:, None] * point[None, :] % nfft) * (2.0 * math.pi / nfft)
    scale = 1.0 / math.sqrt(nfft)
    table = np.stack([np.cos(phase) * scale, -np.sin(phase) * scale], axis=1)
    return table.reshape(2 * channels, nfft).astype(np.float32).astype(jnp.bfloat16)


def correlate_einsum(blocks, frames_all):
    groups_in = blocks.shape[0]
    count = blocks.shape[2]
    local_inputs = blocks.shape[4]
    inputs_all = groups_in * local_inputs
    gram = jnp.einsum("ptcraf,qtcsbf->crpasqb", blocks, blocks, preferred_element_type=jnp.float32)
    gram = gram.reshape(count, 2, inputs_all, 2, inputs_all)
    real_part = (gram[:, 0, :, 0, :] + gram[:, 1, :, 1, :]) / frames_all
    imag_part = (gram[:, 1, :, 0, :] - gram[:, 0, :, 1, :]) / frames_all
    return jnp.stack([real_part, imag_part], axis=1)


def plain_plan(samples, eq_gain):
    local_inputs, local_frames, nfft = samples.shape
    channels = nfft // 2
    n_inp = lax.axis_size("inp")
    n_time = lax.axis_size("tm")
    groups = n_inp * n_time
    chan_dev = channels // groups
    frames_all = n_time * local_frames
    tail = samples[:, local_frames - (TAPS - 1) :, :]
    before = passed_along(tail, "tm", 1)
    padded = jnp.concatenate([before, samples], axis=1)
    window = window_table(TAPS, nfft)
    filtered = jnp.zeros((local_inputs, local_frames, nfft), jnp.float32)
    for tap in range(TAPS):
        filtered = filtered + window[tap] * padded[:, tap : tap + local_frames, :].astype(
            jnp.float32
        )
    filtered = filtered.astype(jnp.bfloat16)
    table = jnp.asarray(fourier_table(channels, nfft))
    spectra = lax.dot_general(
        table, filtered, (((1,), (2,)), ((), ())), preferred_element_type=jnp.float32
    )
    spectra = spectra.reshape(channels, 2, local_inputs, local_frames) * eq_gain[:, None, :, None]
    spectra = spectra.astype(jnp.bfloat16)
    parcel = spectra.reshape(1, groups, chan_dev, 2, local_inputs, local_frames)
    arrived = lax.all_to_all(parcel, ("inp", "tm"), split_axis=1, concat_axis=0, tiled=True)
    count = arrived.shape[2]
    blocks = arrived.reshape(n_inp, n_time, count, 2, local_inputs, local_frames)
    return correlate_einsum(blocks, frames_all)


def spread_kernel(
    n_inp, n_time,
    x_hbm, gain_ref, table_ref, window_ref,
    recv_hbm, late_far_hbm, late_farther_hbm,
    xbuf, turned, tail, taps_buf, halo_out, halo_in, filt, freq, send,
    load_sem, send_sem, recv_sem, halo_send_sem, halo_recv_sem, own_sem, late_sem,
):
    groups = n_inp * n_time
    inputs, frames, nfft = x_hbm.shape
    rows_all = table_ref.shape[0]
    rows_plane = rows_all // n_inp
    rows_dev = rows_all // groups
    pitch = freq.shape[0] // STEP
    steps = frames // STEP
    tiles = nfft // LANES
    keep = TAPS - 1
    z = lax.axis_index("inp")
    t = lax.axis_index("tm")
    me = z * n_time + t

    def load(step):
        f0 = pl.multiple_of(step * STEP, STEP)
        slot = lax.rem(step, 2)
        return pltpu.make_async_copy(
            x_hbm.at[:, pl.ds(f0, STEP), :], xbuf.at[slot], load_sem.at[slot]
        )

    load(steps - 1).start()
    load(steps - 2).start()
    barrier = pltpu.get_barrier_semaphore()

    @pl.loop(1, groups)
    def _(s):
        d = lax.rem(me + s, groups)
        pl.semaphore_signal(
            barrier, inc=1, device_id=(d // n_time, lax.rem(d, n_time)),
            device_id_type=pl.DeviceIdType.MESH,
        )

    rows_late = late_far_hbm.shape[0]
    rows_first = rows_dev - rows_late

    def send_one(step, d_z, s, count=rows_dev):
        d_t = lax.rem(t + s, n_time)
        f0 = pl.multiple_of(step * STEP, STEP)
        d = d_z * n_time + d_t
        r0 = pl.multiple_of(d * rows_dev, rows_dev)
        pltpu.make_async_remote_copy(
            src_ref=send.at[pl.ds(r0, count), pl.ds(f0, STEP), :],
            dst_ref=recv_hbm.at[me, pl.ds(0, count), pl.ds(f0, STEP), :],
            send_sem=send_sem.at[d],
            recv_sem=recv_sem.at[me],
            device_id=(d_z, d_t),
            device_id_type=pl.DeviceIdType.MESH,
        ).start()

    def halo():
        return pltpu.make_async_remote_copy(
            src_ref=halo_out,
            dst_ref=halo_in,
            send_sem=halo_send_sem,
            recv_sem=halo_recv_sem,
            device_id=(z, lax.rem(t + 1, n_time)),
            device_id_type=pl.DeviceIdType.MESH,
        )

    def filter_step(step):
        slot = lax.rem(step, 2)

        @pl.loop(0, tiles)
        def _(tile):
            lanes = pl.ds(pl.multiple_of(tile * LANES, LANES), LANES)
            turned[...] = (
                xbuf[slot, :, :, lanes].astype(jnp.float32).reshape(inputs * STEP, LANES)
            )

            @pl.when(step > 0)
            def _():
                earlier = xbuf[1 - slot, :, :, lanes].astype(jnp.float32)[:, STEP - 8 :, :]
                tail[...] = earlier.reshape(inputs * 8, LANES)
                for k in range(keep):
                    taps_buf[k] = tail[pl.ds(8 - keep + k, inputs, stride=8), :]

            @pl.when(step == 0)
            def _():
                taps_buf[...] = halo_in[:, :, lanes].astype(jnp.float32)

            @pl.when(step == steps - 1)
            def _():
                for k in range(keep):
                    last = turned[pl.ds(STEP - keep + k, inputs, stride=STEP), :]
                    halo_out[k, :, lanes] = last.astype(jnp.bfloat16)

            some = 32
            weights = [
                jnp.broadcast_to(window_ref[tap : tap + 1, lanes], (some, LANES))
                for tap in range(TAPS)
            ]
            for i0 in range(0, inputs, some):
                held = [taps_buf[k, i0 : i0 + some] for k in range(keep)]
                for f in range(STEP):
                    held.append(turned[pl.ds(i0 * STEP + f, some, stride=STEP), :])
                    total = weights[0] * held[0]
                    for tap in range(1, TAPS):
                        total = total + weights[tap] * held[tap]
                    filt[f * inputs + i0 : f * inputs + i0 + some, lanes] = total.astype(
                        jnp.bfloat16
                    )
                    held.pop(0)

    def transform(step, plane):
        f0 = pl.multiple_of(step * STEP, STEP)
        base = pl.multiple_of(plane * rows_plane, rows_plane)
        width = 4

        @pl.loop(0, STEP // width)
        def _(j):
            some = filt[pl.ds(pl.multiple_of(j * width * inputs, width * inputs), width * inputs), :]
            got = lax.dot_general(
                table_ref[pl.ds(base, rows_plane), :], some,
                (((1,), (1,)), ((), ())), preferred_element_type=jnp.float32,
            )
            for w in range(width):
                at = pl.multiple_of((j * width + w) * pitch, 8)
                freq[pl.ds(at, rows_plane), :] = got[:, w * inputs : (w + 1) * inputs]

        @pl.loop(0, rows_plane // 8)
        def _(i):
            for k in range(8):
                row = i * 8 + k
                chan = plane * (rows_plane // 2) + i * 4 + k // 2
                value = freq[pl.ds(row, STEP, stride=pitch), :] * gain_ref[pl.ds(chan, 1), :]
                send[base + row, pl.ds(f0, STEP), :] = value.astype(jnp.bfloat16)

    far = lax.rem(z + 2, 4)
    farther = 3 - z
    near = z + 1 - 2 * lax.rem(z, 2)
    half = n_time // 2

    @pl.loop(0, steps)
    def _(turn):
        step = steps - 1 - turn

        @pl.when(turn == 0)
        def _():
            load(steps - 1).wait()

        @pl.when(step > 0)
        def _():
            load(step - 1).wait()

        @pl.when(step == 0)
        def _():
            @pl.when(t > 0)
            def _():
                halo().wait_recv()

            @pl.when(t == 0)
            def _():
                halo_in[...] = jnp.zeros_like(halo_in)

        filter_step(step)

        @pl.when(step > 1)
        def _():
            load(step - 2).start()

        transform(step, far)

        @pl.when(turn == 0)
        def _():
            pl.semaphore_wait(barrier, groups - 1)

            @pl.when(t < n_time - 1)
            def _():
                halo().start()

        send_one(step, far, 0, rows_first)

        @pl.loop(1, half)
        def _(s):
            send_one(step, far, s)

        transform(step, z)

        @pl.loop(0, half)
        def _(s):
            send_one(step, far, s + half)
            send_one(step, z, s + half)

            @pl.when(s > 0)
            def _():
                send_one(step, z, s)

        transform(step, near)
        transform(step, farther)

        send_one(step, near, 0)
        send_one(step, farther, 0, rows_first)

        @pl.loop(1, n_time)
        def _(s):
            send_one(step, near, s)
            send_one(step, farther, s)

    own = pltpu.make_async_copy(
        send.at[pl.ds(pl.multiple_of(me * rows_dev, rows_dev), rows_dev)], recv_hbm.at[me], own_sem
    )
    own.start()
    partners = (far * n_time + t, farther * n_time + t)
    late = [
        pltpu.make_async_copy(
            send.at[pl.ds(partner * rows_dev + rows_first, rows_late)], late_hbm, late_sem.at[k]
        )
        for k, (partner, late_hbm) in enumerate(zip(partners, (late_far_hbm, late_farther_hbm)))
    ]
    for copy in late:
        copy.start()
    own.wait()
    for copy in late:
        copy.wait()

    @pl.when(t < n_time - 1)
    def _():
        halo().wait_send()

    def finish(d, count):
        gone = send.at[pl.ds(pl.multiple_of(d * rows_dev, rows_dev), count)]
        pltpu.make_async_copy(gone, gone, send_sem.at[d]).wait()
        here = recv_hbm.at[d, pl.ds(0, count)]
        pltpu.make_async_copy(here, here, recv_sem.at[d]).wait()

    @pl.loop(1, groups)
    def _(s):
        d = lax.rem(me + s, groups)

        @pl.when((d == partners[0]) | (d == partners[1]))
        def _():
            finish(d, rows_first)

        @pl.when((d != partners[0]) & (d != partners[1]))
        def _():
            finish(d, rows_dev)


def spread(samples, eq_gain, n_inp, n_time, late):
    inputs, frames, nfft = samples.shape
    channels = nfft // 2
    rows = 2 * channels
    groups = n_inp * n_time
    pitch = rows // n_inp + 8
    vmem = pl.BlockSpec(memory_space=pltpu.VMEM)
    anywhere = pl.BlockSpec(memory_space=pl.ANY)
    return pl.pallas_call(
        functools.partial(spread_kernel, n_inp, n_time),
        out_shape=[
            jax.ShapeDtypeStruct((groups, rows // groups, frames, inputs), jnp.bfloat16),
            jax.ShapeDtypeStruct((2 * late, frames, inputs), jnp.bfloat16),
            jax.ShapeDtypeStruct((2 * late, frames, inputs), jnp.bfloat16),
        ],
        in_specs=[anywhere, vmem, vmem, vmem],
        out_specs=[anywhere] * 3,
        scratch_shapes=[
            pltpu.VMEM((2, inputs, STEP, nfft), jnp.bfloat16),
            pltpu.VMEM((inputs * STEP, LANES), jnp.float32),
            pltpu.VMEM((inputs * 8, LANES), jnp.float32),
            pltpu.VMEM((TAPS - 1, inputs, LANES), jnp.float32),
            pltpu.VMEM((TAPS - 1, inputs, nfft), jnp.bfloat16),
            pltpu.VMEM((TAPS - 1, inputs, nfft), jnp.bfloat16),
            pltpu.VMEM((STEP * inputs, nfft), jnp.bfloat16),
            pltpu.VMEM((STEP * pitch, LANES), jnp.float32),
            pltpu.VMEM((rows, frames, inputs), jnp.bfloat16),
            pltpu.SemaphoreType.DMA((2,)),
            pltpu.SemaphoreType.DMA((groups,)),
            pltpu.SemaphoreType.DMA((groups,)),
            pltpu.SemaphoreType.DMA,
            pltpu.SemaphoreType.DMA,
            pltpu.SemaphoreType.DMA,
            pltpu.SemaphoreType.DMA((2,)),
        ],
        compiler_params=pltpu.CompilerParams(
            collective_id=0, has_side_effects=True, vmem_limit_bytes=56 * 1024 * 1024
        ),
        cost_estimate=pl.CostEstimate(
            flops=2 * rows * nfft * inputs * frames,
            bytes_accessed=4 * inputs * frames * nfft,
            transcendentals=0,
        ),
        name="filter_transform_spread",
    )(
        samples, eq_gain,
        jnp.asarray(fourier_table(channels, nfft)), jnp.asarray(window_table(TAPS, nfft)),
    )


def correlate_kernel(n_inp, scale, block_ref, *refs):
    late_refs = refs[:-1]
    out_ref = refs[-1]
    sources, rows, frames, inputs = block_ref.shape
    n_time = sources // n_inp
    half = n_inp * inputs // 2
    if late_refs:
        z, t = lax.axis_index("inp"), lax.axis_index("tm")
        partners = (lax.rem(z + 2, 4) * n_time + t, (3 - z) * n_time + t)

    def from_source(src, row):
        value = block_ref[src, row]
        if late_refs:
            for partner, late_ref in zip(partners, late_refs):
                value = jnp.where(partner == src, late_ref[row], value)
        return value

    def part(row):
        pieces = [
            jnp.concatenate([from_source(p * n_time + q, row) for q in range(n_time)], axis=0)
            for p in range(n_inp)
        ]
        return jnp.concatenate(pieces, axis=1)

    chans = []
    for chan in range(rows // 2):
        real, imag = part(2 * chan), part(2 * chan + 1)
        chans.append((real, imag, real.T, imag.T))

    def mirror(chan, kind, corner):
        corner = corner.T
        out_ref[chan, kind, half:, 0:half] = -corner if kind else corner

    waiting = None
    for chan, (real, imag, real_t, imag_t) in enumerate(chans):
        right = jnp.concatenate([real, imag], axis=0)
        for kind in range(2):
            left = jnp.concatenate([imag_t, -real_t] if kind else [real_t, imag_t], axis=1)
            upper = jnp.dot(left[:half], right, preferred_element_type=jnp.float32) * scale
            out_ref[chan, kind, 0:half, :] = upper
            if waiting is not None:
                mirror(*waiting)
            waiting = (chan, kind, upper[:, half:])
            out_ref[chan, kind, half:, half:] = (
                jnp.dot(left[half:], right[:, half:], preferred_element_type=jnp.float32) * scale
            )
    mirror(*waiting)


def correlate(arrived, n_inp, late_chans, late=(), before=None):
    sources, rows, frames, inputs = arrived.shape
    count = rows // 2
    inputs_all = n_inp * inputs
    frames_all = sources // n_inp * frames
    turns = (count - late_chans if before is None else late_chans) // 2
    first = 0 if before is None else (count - late_chans) // 2
    in_specs = [pl.BlockSpec((sources, 4, frames, inputs), lambda c: (0, c + first, 0, 0))]
    operands = [arrived]
    aliases = {}
    body = functools.partial(correlate_kernel, n_inp, 1.0 / frames_all)
    if before is not None:
        in_specs += [pl.BlockSpec((4, frames, inputs), lambda c: (c, 0, 0)) for _ in late]
        in_specs.append(pl.BlockSpec(memory_space=pl.ANY))
        operands += [*late, before]
        aliases = {len(operands) - 1: 0}
        whole = body
        body = lambda *refs: whole(*refs[:-2], refs[-1])
    return pl.pallas_call(
        body,
        grid=(turns,),
        out_shape=jax.ShapeDtypeStruct((count, 2, inputs_all, inputs_all), jnp.float32),
        in_specs=in_specs,
        out_specs=pl.BlockSpec((2, 2, inputs_all, inputs_all), lambda c: (c + first, 0, 0, 0)),
        input_output_aliases=aliases,
        compiler_params=pltpu.CompilerParams(vmem_limit_bytes=48 * 1024 * 1024),
        cost_estimate=pl.CostEstimate(
            flops=turns * 12 * inputs_all * inputs_all * frames_all,
            bytes_accessed=turns * (4 * arrived.size // count + 16 * inputs_all * inputs_all),
            transcendentals=0,
        ),
        name="correlate_first" if before is None else "correlate_second",
    )(*operands)


def on_device(samples, eq_gain):
    local_inputs, local_frames, nfft = samples.shape
    n_inp = lax.axis_size("inp")
    n_time = lax.axis_size("tm")
    if local_inputs != LANES or n_inp != 4 or n_time != 8 or local_frames % STEP or local_frames < 2 * STEP or nfft != 1024:
        return plain_plan(samples, eq_gain)
    late_chans = nfft // 2 // (n_inp * n_time) * 3 // 8
    arrived, far, farther = spread(samples, eq_gain, n_inp, n_time, late_chans)
    far = lax.ppermute(far, "inp", [(i, (i + 2) % n_inp) for i in range(n_inp)])
    farther = lax.ppermute(farther, "inp", [(i, n_inp - 1 - i) for i in range(n_inp)])
    first = correlate(arrived, n_inp, late_chans)
    return correlate(arrived, n_inp, late_chans, (far, farther), first)


def solution(mesh):
    placed = (P("inp", "tm", None), P(None, "inp"))
    return jax.shard_map(
        on_device,
        mesh=mesh,
        in_specs=placed,
        out_specs=P(("inp", "tm"), None, None, None),
        check_vma=False,
    )
```
